32 devices in a mesh: patch: 8 (over z, y), sub: 4 (over x, core).
Axes of the slice: x: 2, y: 2, z: 4, core: 2. Of those that a mesh axis runs over, the one named last changes fastest.
Arguments:
- fine_nodes: bfloat16 [16384, 512], P(('patch', 'sub')), may hold values from -6 to 6
- coarse_nodes: bfloat16 [128, 512], replicated, may hold values from -6 to 6
- neighbours: int32 [6, 16384], P(None, ('patch', 'sub')), may hold values from 0 to 768, as said below
- send_rows: int32 [32, 2, 128], P(('patch', 'sub')), may hold values from 0 to 511, as said below
- real_rows: int32 [32], P(('patch', 'sub')), may hold values from 256 to 512
- parent: int32 [16384], P(('patch', 'sub')), may hold values from 0 to 127
- coarse_edges: int32 [2, 4096], P(None, ('patch', 'sub')), may hold values from 0 to 127
- coarse_live: int32 [32], P(('patch', 'sub')), may hold values from 32 to 128
- msg_weight: bfloat16 [1024, 512], replicated, may hold values from -0.1875 to 0.1875
- msg_bias: float32 [512], replicated, may hold values from -3 to 3
- node_weight: bfloat16 [1536, 512], replicated, may hold values from -0.15625 to 0.15625
- node_bias: float32 [512], replicated, may hold values from -3 to 3
- coarse_msg_weight: bfloat16 [1024, 512], replicated, may hold values from -0.1875 to 0.1875
- coarse_msg_bias: float32 [512], replicated, may hold values from -3 to 3
- coarse_node_weight: bfloat16 [1024, 512], replicated, may hold values from -0.1875 to 0.1875
- coarse_node_bias: float32 [512], replicated, may hold values from -3 to 3
- out_grad: bfloat16 [16384, 512], P(('patch', 'sub')), may hold values from -6 to 6
Outputs:
- new_fine: bfloat16 [16384, 512], P(('patch', 'sub'))
- new_coarse: bfloat16 [128, 512], replicated
- node_grad: bfloat16 [16384, 512], P(('patch', 'sub'))
- msg_weight_grad: float32 [1024, 512], replicated
The draws below stay inside these ranges and needn't reach their ends.
Inputs may be any that keep to these rules, and one draw needn't show every extreme that they name: `neighbours`: entry [k, i] of device d is a real local row below real_rows[d], 512 + j for row j of the 128 received from the previous device, 640 + j for row j of those from the next one, or 768 for an empty slot. Padding rows have only empty slots, and every real row has 4 or more filled slots. `send_rows`: each entry is a real row of the sending device; rows may repeat.
All inputs are finite; a program needn't handle non-finite values.
Results may differ from the reference program's by a relative error of at most 0.0071.
Values may be sent and summed in bfloat16 or wider, within the bound.
A program may use at most 64 MiB of HBM per device.

```python
import jax
import jax.numpy as jnp
from jax import lax

WIDTH = 512
NODE_DEV = 512
SEND = 128
DEG = 6
CE_DEV = 128
DEVICE_COUNT = 32
NODES = 16384
CN = 128
CE = 4096


def live_counts(key):
    device_total = NODES // NODE_DEV
    counts = NODE_DEV // 2 + jax.random.randint(key, (device_total,), 0, NODE_DEV // 2 + 1)
    return counts.at[0].set(NODE_DEV).at[1].set(NODE_DEV // 2).astype(jnp.int32)


def draw_real_rows(key, part):
    return live_counts(key)


def draw_neighbours(key, part):
    counts = live_counts(key)
    key = jax.random.fold_in(key, 11)
    key_local, key_halo, key_kind, key_fill = jax.random.split(key, 4)
    device_total = NODES // NODE_DEV
    grid_shape = (DEG, device_total, NODE_DEV)
    local_pick = jax.random.randint(key_local, grid_shape, 0, 1 << 20) % counts[None, :, None]
    halo_pick = NODE_DEV + jax.random.randint(key_halo, grid_shape, 0, 2 * SEND)
    use_halo = jax.random.randint(key_kind, grid_shape, 0, 3) == 0
    filled_count = jax.random.randint(key_fill, (1, device_total, NODE_DEV), 4, DEG + 1)
    slot_index = jnp.arange(DEG)[:, None, None]
    node_index = jnp.arange(NODE_DEV)[None, None, :]
    active = (slot_index < filled_count) & (node_index < counts[None, :, None])
    chosen = jnp.where(use_halo, halo_pick, local_pick)
    return jnp.where(active, chosen, NODE_DEV + 2 * SEND).reshape(DEG, NODES).astype(jnp.int32)


def draw_send_rows(key, part):
    counts = live_counts(key)
    key = jax.random.fold_in(key, 12)
    device_total = NODES // NODE_DEV
    listed = jax.random.randint(key, (device_total, 2, SEND), 0, 1 << 20) % counts[:, None, None]
    return listed.at[0, 0, 0].set(NODE_DEV - 1).at[0, 1, 0].set(0).astype(jnp.int32)


def draw_coarse_live(key, part):
    key = jax.random.fold_in(key, 13)
    device_total = NODES // NODE_DEV
    lowest = CE_DEV // 4
    counts = jax.random.randint(key, (device_total,), lowest, CE_DEV + 1)
    return counts.at[0].set(CE_DEV).at[1].set(lowest).astype(jnp.int32)


def touch_ends(values, stream_key, smallest, top_value):
    shape = values.shape
    index_at = [jax.random.randint(jax.random.fold_in(stream_key, axis), (), 0, shape[axis]) for axis in range(len(shape))]
    values = values.at[tuple(index_at)].set(smallest)
    longest = shape.index(max(shape))
    index_at[longest] = (index_at[longest] + 1) % shape[longest]
    return values.at[tuple(index_at)].set(top_value)


def block_levels(rng, shape, cuts, smallest, high):
    def one(axis_at, blocks):
        steps = jax.random.uniform(jax.random.fold_in(jax.random.fold_in(rng, 6), axis_at), (blocks,), jnp.float32, smallest / len(cuts), high / len(cuts))
        return jnp.repeat(jnp.exp(steps), shape[axis_at] // blocks).reshape((-1,) + (1,) * (len(shape) - axis_at - 1))

    level = one(*cuts[0])
    for cut in cuts[1:]:
        level = level * one(*cut)
    return level


def normal_values(own_key, shape, width, most, shards=(), held_as=jnp.bfloat16):
    entries = width * jax.random.normal(own_key, shape, jnp.float32)
    if shards:
        entries = entries * block_levels(own_key, shape, shards, -0.22, 0.18)
    return jnp.clip(entries, -most, most).astype(held_as)


def setup_inputs(seed: int = 0) -> dict:
    key_list = jax.random.split(jax.random.key(seed), 18)
    return {
        "fine_nodes": normal_values(key_list[0], (NODES, WIDTH), 1.0, 6.0, ((0, 32),)),
        "coarse_nodes": normal_values(key_list[1], (CN, WIDTH), 1.0, 6.0),
        "neighbours": draw_neighbours(jax.random.fold_in(key_list[17], 71), 0),
        "send_rows": draw_send_rows(jax.random.fold_in(key_list[17], 71), 0),
        "real_rows": draw_real_rows(jax.random.fold_in(key_list[17], 71), 0),
        "parent": touch_ends(jax.random.randint(key_list[5], (NODES,), 0, CN), jax.random.fold_in(key_list[5], 1), 0, CN - 1).astype(jnp.int32),
        "coarse_edges": touch_ends(jax.random.randint(key_list[6], (2, CE), 0, CN), jax.random.fold_in(key_list[6], 1), 0, CN - 1).astype(jnp.int32),
        "coarse_live": draw_coarse_live(jax.random.fold_in(key_list[17], 71), 0),
        "msg_weight": normal_values(key_list[8], (2 * WIDTH, WIDTH), (2 * WIDTH) ** -0.5, 0.1875),
        "msg_bias": normal_values(key_list[9], (WIDTH,), 0.5, 3.0, (), jnp.float32),
        "node_weight": normal_values(key_list[10], (3 * WIDTH, WIDTH), (3 * WIDTH) ** -0.5, 0.15625),
        "node_bias": normal_values(key_list[11], (WIDTH,), 0.5, 3.0, (), jnp.float32),
        "coarse_msg_weight": normal_values(key_list[12], (2 * WIDTH, WIDTH), (2 * WIDTH) ** -0.5, 0.1875),
        "coarse_msg_bias": normal_values(key_list[13], (WIDTH,), 0.5, 3.0, (), jnp.float32),
        "coarse_node_weight": normal_values(key_list[14], (2 * WIDTH, WIDTH), (2 * WIDTH) ** -0.5, 0.1875),
        "coarse_node_bias": normal_values(key_list[15], (WIDTH,), 0.5, 3.0, (), jnp.float32),
        "out_grad": normal_values(key_list[16], (NODES, WIDTH), 1.0, 6.0, ((0, 32),)),
    }


epsilon = 1e-06

def slope(values):
    sigmoid_part = jax.nn.sigmoid(values)
    return sigmoid_part * (1.0 + values * (1.0 - sigmoid_part))

def coarse_update(coarse_nodes, coarse_edges, coarse_live, coarse_msg_weight, coarse_msg_bias, coarse_node_weight, coarse_node_bias):
    slot_total = coarse_edges.shape[1]
    slot_index = jnp.arange(slot_total, dtype=jnp.int32) % CE_DEV
    owner_index = jnp.arange(slot_total, dtype=jnp.int32) // CE_DEV
    usable = (slot_index < coarse_live[owner_index]).astype(jnp.float32)
    senders = jnp.take(coarse_nodes, coarse_edges[0], axis=0)
    receivers = jnp.take(coarse_nodes, coarse_edges[1], axis=0)
    coarse_pre = jnp.dot(jnp.concatenate([senders, receivers], 1), coarse_msg_weight, preferred_element_type=jnp.float32) + coarse_msg_bias
    message = (jax.nn.silu(coarse_pre) * usable[:, None]).astype(jnp.bfloat16)
    summed = jax.ops.segment_sum(message.astype(jnp.float32), coarse_edges[1], num_segments=CN).astype(jnp.bfloat16)
    hidden = jnp.dot(jnp.concatenate([coarse_nodes, summed], 1), coarse_node_weight, preferred_element_type=jnp.float32) + coarse_node_bias
    return (coarse_nodes.astype(jnp.float32) + jax.nn.silu(hidden)).astype(jnp.bfloat16)

def reference(fine_nodes, coarse_nodes, neighbours, send_rows, real_rows, parent, coarse_edges, coarse_live, msg_weight, msg_bias, node_weight, node_bias, coarse_msg_weight, coarse_msg_bias, coarse_node_weight, coarse_node_bias, out_grad):
    new_coarse = coarse_update(coarse_nodes, coarse_edges, coarse_live, coarse_msg_weight, coarse_msg_bias, coarse_node_weight, coarse_node_bias)
    device_nodes = fine_nodes.reshape(DEVICE_COUNT, NODE_DEV, WIDTH)
    sent = jax.vmap(lambda rows_here, listed: jnp.take(rows_here, listed, axis=0))(device_nodes, send_rows.reshape(DEVICE_COUNT, 2 * SEND))
    from_prev = jnp.roll(sent[:, SEND:], 1, 0)
    from_next = jnp.roll(sent[:, :SEND], -1, 0)
    lookup = jnp.concatenate([device_nodes, from_prev, from_next], 1)
    device_links = neighbours.reshape(DEG, DEVICE_COUNT, NODE_DEV).transpose(1, 0, 2)
    lifted = jnp.take(new_coarse, parent, axis=0).reshape(DEVICE_COUNT, NODE_DEV, WIDTH)
    cotangent = out_grad.reshape(DEVICE_COUNT, NODE_DEV, WIDTH)
    source_weight = msg_weight[:WIDTH]
    target_weight = msg_weight[WIDTH:]
    table_rows = NODE_DEV + 2 * SEND

    def one_device(device_inputs):
        nodes_here, table_here, links_here, live_here, lifted_here, cotangent_here = device_inputs
        source_proj = jnp.dot(table_here, source_weight, preferred_element_type=jnp.float32)
        source_proj = jnp.concatenate([source_proj, jnp.zeros((1, WIDTH), jnp.float32)], 0)
        target_proj = jnp.dot(nodes_here, target_weight, preferred_element_type=jnp.float32)
        edge_pre = jnp.take(source_proj, links_here, axis=0) + target_proj[None] + msg_bias
        filled = (links_here < table_rows).astype(jnp.float32)[..., None]
        aggregated = lax.optimization_barrier(jnp.sum(jax.nn.silu(edge_pre) * filled, axis=0)).astype(jnp.bfloat16)
        is_real = (jnp.arange(NODE_DEV, dtype=jnp.int32) < live_here)[:, None]
        joined = jnp.concatenate([nodes_here, aggregated, lifted_here], 1)
        node_pre = jnp.dot(joined, node_weight, preferred_element_type=jnp.float32) + node_bias
        new_rows = jnp.where(is_real, nodes_here.astype(jnp.float32) + jax.nn.silu(node_pre), 0.0).astype(jnp.bfloat16)
        node_delta = jnp.where(is_real, cotangent_here.astype(jnp.float32) * slope(node_pre), 0.0).astype(jnp.bfloat16)
        node_back = jnp.dot(node_delta, node_weight.T, preferred_element_type=jnp.float32)
        edge_delta = (node_back[None, :, WIDTH:2 * WIDTH] * slope(edge_pre) * filled).astype(jnp.bfloat16)
        delta_sum = lax.optimization_barrier(jnp.sum(edge_delta.astype(jnp.float32), axis=0)).astype(jnp.bfloat16)
        table_delta = jax.ops.segment_sum(edge_delta.reshape(-1, WIDTH).astype(jnp.float32), links_here.reshape(-1), num_segments=table_rows + 1)[:table_rows].astype(jnp.bfloat16)
        table_grad = jnp.dot(table_delta, source_weight.T, preferred_element_type=jnp.float32)
        local_grad = cotangent_here.astype(jnp.float32) + node_back[:, :WIDTH] + jnp.dot(delta_sum, target_weight.T, preferred_element_type=jnp.float32) + table_grad[:NODE_DEV]
        grad_source = jnp.dot(table_here.T, table_delta, preferred_element_type=jnp.float32)
        grad_target = jnp.dot(nodes_here.T, delta_sum, preferred_element_type=jnp.float32)
        return (new_rows, local_grad, table_grad[NODE_DEV:], jnp.concatenate([grad_source, grad_target], 0))
    new_rows, local_grad, rim_grad, grad_parts = lax.map(one_device, (device_nodes, lookup, device_links, real_rows, lifted, cotangent))
    to_prev_grad = jnp.roll(rim_grad[:, SEND:], 1, 0)
    to_next_grad = jnp.roll(rim_grad[:, :SEND], -1, 0)

    def scatter_back(listed, grad_prev, grad_next):
        base = jnp.zeros((NODE_DEV, WIDTH), jnp.float32)
        return base.at[listed[0]].add(grad_prev).at[listed[1]].add(grad_next)
    returned = jax.vmap(scatter_back)(send_rows, to_prev_grad, to_next_grad)
    is_real = (jnp.arange(NODE_DEV, dtype=jnp.int32)[None, :] < real_rows[:, None])[..., None]
    node_grad = jnp.where(is_real, local_grad + returned, 0.0).astype(jnp.bfloat16).reshape(NODES, WIDTH)
    raw_grad = lax.optimization_barrier(jnp.sum(grad_parts, axis=0))
    factor = lax.rsqrt(jnp.mean(raw_grad * raw_grad) + epsilon)
    return (new_rows.reshape(NODES, WIDTH), new_coarse, node_grad, raw_grad * factor)
```

```python
import functools

import jax
import jax.numpy as jnp
from jax import lax
from jax.experimental import pallas as pl
from jax.experimental.pallas import tpu as pltpu
from jax.sharding import PartitionSpec as P

MESH = pl.DeviceIdType.MESH
AXES = ("patch", "sub")
epsilon = 1e-06
BF = jnp.bfloat16
F32 = jnp.float32


def mm(a, b):
    return jnp.dot(a, b, preferred_element_type=F32)


def mm_nt(a, b):
    return lax.dot_general(a, b, (((1,), (1,)), ((), ())), preferred_element_type=F32)


def mm_tn(a, b):
    return lax.dot_general(a, b, (((0,), (0,)), ((), ())), preferred_element_type=F32)


def sigmoid(v):
    return 0.5 + 0.5 * jnp.tanh(0.5 * v)


def onehot_rows(count, row):
    at = lax.broadcasted_iota(jnp.int32, (count, row.shape[1]), 0)
    return jnp.where(at == row, 1.0, 0.0).astype(BF)


def layer_kernel(
    patches, subs, cut,
    real_ref, live_ref, nb_ref, send_ref, parent_ref, edges_ref, coarse_ref,
    mbias_ref, nbias_ref, cmbias_ref, cnbias_ref,
    fine_hbm, msgw_hbm, nodew_hbm, cmw_hbm, cnw_hbm, og_hbm,
    newfine_ref, newcoarse_ref, nodegrad_ref, raw_hbm, factor_ref,
    lookup, msgw, nodew, cmw, cnw, og, load_sem,
    outgoing, ret, retout, halo_ssem, halo_rsem,
    cbuf, crecv, cag, c_sem,
    pick, slopes, edelta, source, tdelta, dsum, local, sends_oh,
    gbuf, recv_a, sum_b, recv_b, ag, g_sem, out_sem,
):
    n = patches * subs
    half = n // 2
    rows, width = og.shape
    send = outgoing.shape[1]
    table = lookup.shape[0]
    deg = nb_ref.shape[0]
    cn = coarse_ref.shape[0]
    _, _, rpc, cpc = gbuf.shape
    crow, ccol = cbuf.shape[1:]
    me = lax.axis_index("patch") * subs + lax.axis_index("sub")
    par = lax.rem(me, 2)
    group = lax.div(me, 2)

    def dev(i):
        return (lax.div(i, subs), lax.rem(i, subs))

    partner = dev(me + 1 - 2 * par)
    nxt, prv = dev(lax.rem(me + 1, n)), dev(lax.rem(me + n - 1, n))

    def remote(src, dst, ssem, rsem, to):
        return pltpu.make_async_remote_copy(
            src_ref=src, dst_ref=dst, send_sem=ssem, recv_sem=rsem,
            device_id=to, device_id_type=MESH,
        )

    barrier = pltpu.get_barrier_semaphore()

    def greet(o, c):
        pl.semaphore_signal(barrier, inc=1, device_id=dev(lax.rem(me + o, n)), device_id_type=MESH)
        return c

    loads = [
        pltpu.make_async_copy(fine_hbm, lookup.at[pl.ds(0, rows)], load_sem.at[0]),
        pltpu.make_async_copy(cmw_hbm, cmw, load_sem.at[1]),
        pltpu.make_async_copy(msgw_hbm, msgw, load_sem.at[2]),
        pltpu.make_async_copy(nodew_hbm, nodew, load_sem.at[3]),
        pltpu.make_async_copy(cnw_hbm, cnw, load_sem.at[4]),
        pltpu.make_async_copy(og_hbm, og, load_sem.at[5]),
    ]
    for load in loads:
        load.start()
    lax.fori_loop(1, n, greet, 0)

    sends_oh[:, :send] = onehot_rows(rows, send_ref[0:1, :])
    sends_oh[:, send:] = onehot_rows(rows, send_ref[1:2, :])
    loads[0].wait()
    fine = lookup[pl.ds(0, rows), :]
    gathered = mm_tn(sends_oh[...], fine).astype(BF)
    outgoing[0] = gathered[:send]
    outgoing[1] = gathered[send:]
    pl.semaphore_wait(barrier, n - 1)
    halo = [
        remote(outgoing.at[1], lookup.at[pl.ds(rows, send)], halo_ssem.at[0], halo_rsem.at[0], nxt),
        remote(outgoing.at[0], lookup.at[pl.ds(rows + send, send)], halo_ssem.at[1], halo_rsem.at[1], prv),
    ]
    for copy in halo:
        copy.start()

    coarse = coarse_ref[...]
    to_sender = onehot_rows(cn, edges_ref[0:1, :])
    to_receiver = onehot_rows(cn, edges_ref[1:2, :])
    senders = mm_tn(to_sender, coarse).astype(BF)
    receivers = mm_tn(to_receiver, coarse).astype(BF)
    loads[1].wait()
    pre = mm(senders, cmw[:width, :]) + mm(receivers, cmw[width:, :]) + cmbias_ref[...]
    slot = lax.broadcasted_iota(jnp.int32, pre.shape, 0)
    message = jnp.where(slot < live_ref[0], pre * sigmoid(pre), 0.0).astype(BF)
    partial = mm(to_receiver, message).astype(BF)
    blocks = cn // crow
    for cb in range(width // ccol):
        cbuf[pl.ds(cb * blocks, blocks)] = partial[:, cb * ccol:(cb + 1) * ccol].reshape(blocks, crow, ccol)

    def send_partial(o, c):
        to = lax.rem(me + o, n)
        remote(cbuf.at[to], crecv.at[o - 1], c_sem.at[0], c_sem.at[1], dev(to)).start()
        return c

    lax.fori_loop(1, n, send_partial, 0)

    loads[2].wait()
    source[pl.ds(0, rows), :] = mm(fine, msgw[:width, :]).astype(BF)
    target = mm(fine, msgw[width:, :]) + mbias_ref[...]
    local[...] = target
    for k in range(deg):
        pick[:, k * rows:(k + 1) * rows] = onehot_rows(table, nb_ref[k:k + 1, :])

    remote(crecv, crecv, c_sem.at[0], c_sem.at[1], partner).wait_recv()
    share = jnp.sum(crecv[...].astype(F32), axis=0) + cbuf[me].astype(F32)
    cag[me] = share.astype(BF)

    def send_share(o, c):
        remote(cag.at[me], cag.at[me], c_sem.at[2], c_sem.at[3], dev(lax.rem(me + o, n))).start()
        return c

    lax.fori_loop(1, n, send_share, 0)

    for copy in halo:
        copy.wait_recv()
    source[pl.ds(rows, table - rows), :] = mm(lookup[pl.ds(rows, table - rows), :], msgw[:width, :]).astype(BF)
    nb = jnp.concatenate([nb_ref[...], nb_ref[0:8 - deg, :]], 0)
    nb_col = nb.astype(F32).T.astype(jnp.int32)
    tile = rows // 2
    parts = []
    for t in range(2):
        agg = jnp.zeros((tile, width), F32)
        tgt = local[pl.ds(t * tile, tile), :]
        at = lax.broadcasted_iota(jnp.int32, (tile, table), 1)
        for k in range(deg):
            col = nb_col[t * tile:(t + 1) * tile, k:k + 1]
            hot = jnp.where(at == col, 1.0, 0.0).astype(BF)
            v = mm(hot, source[...]) + tgt
            filled = jnp.where(col < table, 1.0, 0.0)
            s = sigmoid(v) * filled
            silu = v * s
            agg = agg + silu
            slopes[k, pl.ds(t * tile, tile), :] = s + silu * (1.0 - s)
        parts.append(agg.astype(BF))
    aggregated = jnp.concatenate(parts, 0)

    loads[3].wait()
    first = mm(fine, nodew[:width, :]) + mm(aggregated, nodew[width:2 * width, :]) + nbias_ref[...]
    loads[4].wait()
    remote(crecv, crecv, c_sem.at[2], c_sem.at[3], partner).wait_recv()
    summed = jnp.concatenate(
        [cag[pl.ds(cb * blocks, blocks)].reshape(cn, ccol) for cb in range(width // ccol)], 1
    )
    hidden = mm(coarse, cnw[:width, :]) + mm(summed, cnw[width:, :]) + cnbias_ref[...]
    new_coarse = (coarse.astype(F32) + hidden * sigmoid(hidden)).astype(BF)
    newcoarse_ref[...] = new_coarse

    lifted = mm_tn(onehot_rows(cn, parent_ref[...]), new_coarse).astype(BF)
    node_pre = first + mm(lifted, nodew[2 * width:, :])
    real = lax.broadcasted_iota(jnp.int32, (rows, width), 0) < real_ref[0]
    s = sigmoid(node_pre)
    silu = node_pre * s
    newfine_ref[...] = jnp.where(real, fine.astype(F32) + silu, 0.0).astype(BF)
    loads[5].wait()
    out_grad = og[...].astype(F32)
    node_delta = jnp.where(real, out_grad * (s + silu * (1.0 - s)), 0.0).astype(BF)
    back = mm_nt(node_delta, nodew[width:2 * width, :])
    total = jnp.zeros((rows, width), F32)
    for k in range(deg):
        ed = (back * slopes[k]).astype(BF)
        edelta[pl.ds(k * rows, rows), :] = ed
        total = total + ed.astype(F32)
    dsum[...] = total.astype(BF)

    tdelta[pl.ds(rows, table - rows), :] = mm(pick[pl.ds(rows, table - rows), :], edelta[...]).astype(BF)
    rim = mm_nt(tdelta[pl.ds(rows, table - rows), :], msgw[:width, :]).astype(BF)
    retout[0] = rim[:send]
    retout[1] = rim[send:]
    give = [
        remote(retout.at[1], ret.at[0], halo_ssem.at[2], halo_rsem.at[2], nxt),
        remote(retout.at[0], ret.at[1], halo_ssem.at[3], halo_rsem.at[3], prv),
    ]
    for copy in give:
        copy.start()
    tdelta[pl.ds(0, rows), :] = mm(pick[pl.ds(0, rows), :], edelta[...]).astype(BF)

    def keep(grad, base):
        for i in range(grad.shape[0] // rpc):
            for j in range(cut):
                c = (base // rpc + i) * cut + j
                gbuf[c % 2, c // 2] = grad[i * rpc:(i + 1) * rpc, j * cpc:(j + 1) * cpc]

    keep(mm_tn(lookup[...], tdelta[...]).astype(BF), 0)
    keep(mm_tn(fine, dsum[...]).astype(BF), width)
    swap = remote(gbuf.at[1 - par], recv_a, g_sem.at[0], g_sem.at[1], partner)
    swap.start()
    local[...] = out_grad + mm_nt(node_delta, nodew[:width, :])
    swap.wait_recv()
    sum_b[...] = (gbuf[par].astype(F32) + recv_a[...].astype(F32)).astype(BF)

    def send_chunk(o, c):
        to = lax.rem(group + o, half)
        remote(sum_b.at[to], recv_b.at[o - 1], g_sem.at[2], g_sem.at[3], dev(2 * to + par)).start()
        return c

    lax.fori_loop(1, half, send_chunk, 0)

    grad = local[...] + mm_nt(dsum[...], msgw[width:, :]) + mm_nt(tdelta[pl.ds(0, rows), :], msgw[:width, :])
    for copy in give:
        copy.wait_recv()
    grad = grad + mm(sends_oh[:, :send], ret[0]) + mm(sends_oh[:, send:], ret[1])
    nodegrad_ref[...] = jnp.where(real, grad, 0.0).astype(BF)

    remote(recv_b, recv_b, g_sem.at[2], g_sem.at[3], partner).wait_recv()
    chunk = jnp.sum(recv_b[...].astype(F32), axis=0) + sum_b[group].astype(F32)
    ag[par, group] = chunk.astype(BF)

    def send_sum(o, c):
        to = lax.rem(group + o, half)
        mine = ag.at[par, group]
        remote(mine, mine, g_sem.at[4], g_sem.at[5], dev(2 * to + par)).start()
        return c

    lax.fori_loop(1, half, send_sum, 0)
    remote(recv_b, recv_b, g_sem.at[4], g_sem.at[5], partner).wait_recv()
    last = remote(ag.at[par], ag.at[par], g_sem.at[6], g_sem.at[7], partner)
    last.start()
    last.wait_recv()
    out = pltpu.make_async_copy(ag, raw_hbm, out_sem)
    out.start()
    raw = ag[...].astype(F32)
    mean = jnp.sum(raw * raw) / (2 * width * width)
    factor_ref[...] = jnp.full(factor_ref.shape, lax.rsqrt(mean + epsilon), F32)

    for copy in halo + give:
        copy.wait_send()
    remote(crecv, crecv, c_sem.at[0], c_sem.at[1], partner).wait_send()
    remote(crecv, crecv, c_sem.at[2], c_sem.at[3], partner).wait_send()
    swap.wait_send()
    remote(recv_b, recv_b, g_sem.at[2], g_sem.at[3], partner).wait_send()
    remote(recv_b, recv_b, g_sem.at[4], g_sem.at[5], partner).wait_send()
    last.wait_send()
    out.wait()


def shards(
    patches, subs,
    fine_nodes, coarse_nodes, neighbours, send_rows, real_rows, parent,
    coarse_edges, coarse_live, msg_weight, msg_bias, node_weight, node_bias,
    coarse_msg_weight, coarse_msg_bias, coarse_node_weight, coarse_node_bias,
    out_grad,
):
    n = patches * subs
    half = n // 2
    rows, width = fine_nodes.shape
    send = send_rows.shape[2]
    table = rows + 2 * send
    deg = neighbours.shape[0]
    cn = coarse_nodes.shape[0]
    cut = max(1, 16 * n // (2 * width))
    rpc, cpc = 2 * width * cut // n, width // cut
    ccol = 128
    crow = cn * (width // ccol) // n
    vmem = pl.BlockSpec(memory_space=pltpu.VMEM)
    smem = pl.BlockSpec(memory_space=pltpu.SMEM)
    hbm = pl.BlockSpec(memory_space=pl.ANY)
    V = pltpu.VMEM
    dma = pltpu.SemaphoreType.DMA
    new_fine, new_coarse, node_grad, raw, factor = pl.pallas_call(
        functools.partial(layer_kernel, patches, subs, cut),
        out_shape=(
            jax.ShapeDtypeStruct((rows, width), BF),
            jax.ShapeDtypeStruct((cn, width), BF),
            jax.ShapeDtypeStruct((rows, width), BF),
            jax.ShapeDtypeStruct((2, half, rpc, cpc), BF),
            jax.ShapeDtypeStruct((8, 128), F32),
        ),
        in_specs=[smem, smem] + [vmem] * 9 + [hbm] * 6,
        out_specs=(vmem, vmem, vmem, hbm, vmem),
        scratch_shapes=[
            V((table, width), BF), V((2 * width, width), BF), V((3 * width, width), BF),
            V((2 * width, width), BF), V((2 * width, width), BF), V((rows, width), BF), dma((6,)),
            V((2, send, width), BF), V((2, send, width), BF), V((2, send, width), BF), dma((4,)), dma((4,)),
            V((n, crow, ccol), BF), V((n - 1, crow, ccol), BF), V((n, crow, ccol), BF), dma((4,)),
            V((table, deg * rows), BF), V((deg, rows, width), F32), V((deg * rows, width), BF),
            V((table, width), BF), V((table, width), BF), V((rows, width), BF),
            V((rows, width), F32), V((rows, 2 * send), BF),
            V((2, half, rpc, cpc), BF), V((half, rpc, cpc), BF), V((half, rpc, cpc), BF),
            V((half - 1, rpc, cpc), BF), V((2, half, rpc, cpc), BF), dma((8,)), dma,
        ],
        compiler_params=pltpu.CompilerParams(
            collective_id=0, has_side_effects=True, vmem_limit_bytes=56 * 1024 * 1024
        ),
        name="layer",
    )(
        real_rows, coarse_live, neighbours, send_rows[0], parent[None, :], coarse_edges, coarse_nodes,
        msg_bias[None, :], node_bias[None, :], coarse_msg_bias[None, :], coarse_node_bias[None, :],
        fine_nodes, msg_weight, node_weight, coarse_msg_weight, coarse_node_weight, out_grad,
    )
    ordered = raw.transpose(1, 0, 2, 3).reshape(2 * width // rpc, cut, rpc, cpc).transpose(0, 2, 1, 3)
    msg_weight_grad = ordered.reshape(2 * width, width).astype(F32) * factor[0, 0]
    return new_fine, new_coarse, node_grad, msg_weight_grad


def solution(mesh):
    both = P(AXES)
    placed = (
        P(AXES, None), P(), P(None, AXES), P(AXES, None, None), both, both, P(None, AXES), both,
        P(), P(), P(), P(), P(), P(), P(), P(), P(AXES, None),
    )
    return jax.shard_map(
        functools.partial(shards, mesh.shape["patch"], mesh.shape["sub"]),
        mesh=mesh,
        in_specs=placed,
        out_specs=(P(AXES, None), P(), P(AXES, None), P()),
        check_vma=False,
    )
```

```python
import functools

import jax
import jax.numpy as jnp
from jax import lax
from jax.experimental import pallas as pl
from jax.experimental.pallas import tpu as pltpu
from jax.sharding import PartitionSpec as P

MESH = pl.DeviceIdType.MESH
AXES = ("patch", "sub")
epsilon = 1e-06
BF = jnp.bfloat16
F32 = jnp.float32


def mm(a, b):
    return jnp.dot(a, b, preferred_element_type=F32)


def mm_nt(a, b):
    return lax.dot_general(a, b, (((1,), (1,)), ((), ())), preferred_element_type=F32)


def mm_tn(a, b):
    return lax.dot_general(a, b, (((0,), (0,)), ((), ())), preferred_element_type=F32)


def sigmoid(v):
    return 0.5 + 0.5 * jnp.tanh(0.5 * v)


def onehot_rows(count, row):
    at = lax.broadcasted_iota(jnp.int32, (count, row.shape[1]), 0)
    return jnp.where(at == row, 1.0, 0.0).astype(BF)


def layer_kernel(
    patches, subs, cut,
    real_ref, live_ref, nb_ref, send_ref, parent_ref, edges_ref, coarse_ref,
    mbias_ref, nbias_ref, cmbias_ref, cnbias_ref,
    fine_hbm, msgw_hbm, nodew_hbm, cmw_hbm, cnw_hbm, og_hbm,
    newfine_ref, newcoarse_ref, nodegrad_ref, raw_hbm, factor_ref,
    lookup, msgw, nodew, cmw, cnw, og, load_sem,
    outgoing, ret, retout, halo_ssem, halo_rsem,
    cbuf, crecv, cag, c_sem,
    pick, slopes, edelta, source, tdelta, dsum, local, sends_oh,
    gbuf, recv_a, sum_b, recv_b, ag, g_sem, ag_sem, out_sem,
):
    n = patches * subs
    half = n // 2
    rows, width = og.shape
    send = outgoing.shape[1]
    table = lookup.shape[0]
    deg = nb_ref.shape[0]
    cn = coarse_ref.shape[0]
    _, _, rpc, cpc = gbuf.shape
    crow, ccol = cbuf.shape[1:]
    me = lax.axis_index("patch") * subs + lax.axis_index("sub")
    par = lax.rem(me, 2)
    group = lax.div(me, 2)

    def dev(i):
        return (lax.div(i, subs), lax.rem(i, subs))

    partner = dev(me + 1 - 2 * par)
    nxt, prv = dev(lax.rem(me + 1, n)), dev(lax.rem(me + n - 1, n))

    def remote(src, dst, ssem, rsem, to):
        return pltpu.make_async_remote_copy(
            src_ref=src, dst_ref=dst, send_sem=ssem, recv_sem=rsem,
            device_id=to, device_id_type=MESH,
        )

    barrier = pltpu.get_barrier_semaphore()

    def greet(o, c):
        pl.semaphore_signal(barrier, inc=1, device_id=dev(lax.rem(me + o, n)), device_id_type=MESH)
        return c

    loads = [
        pltpu.make_async_copy(fine_hbm, lookup.at[pl.ds(0, rows)], load_sem.at[0]),
        pltpu.make_async_copy(cmw_hbm, cmw, load_sem.at[1]),
        pltpu.make_async_copy(msgw_hbm, msgw, load_sem.at[2]),
        pltpu.make_async_copy(nodew_hbm, nodew, load_sem.at[3]),
        pltpu.make_async_copy(cnw_hbm, cnw, load_sem.at[4]),
        pltpu.make_async_copy(og_hbm, og, load_sem.at[5]),
    ]
    for load in loads:
        load.start()
    lax.fori_loop(1, n, greet, 0)

    sends_oh[:, :send] = onehot_rows(rows, send_ref[0:1, :])
    sends_oh[:, send:] = onehot_rows(rows, send_ref[1:2, :])
    loads[0].wait()
    fine = lookup[pl.ds(0, rows), :]
    gathered = mm_tn(sends_oh[...], fine).astype(BF)
    outgoing[0] = gathered[:send]
    outgoing[1] = gathered[send:]
    coarse = coarse_ref[...]
    to_sender = onehot_rows(cn, edges_ref[0:1, :])
    to_receiver = onehot_rows(cn, edges_ref[1:2, :])
    senders = mm_tn(to_sender, coarse).astype(BF)
    receivers = mm_tn(to_receiver, coarse).astype(BF)
    loads[1].wait()
    pre = mm(senders, cmw[:width, :]) + mm(receivers, cmw[width:, :]) + cmbias_ref[...]
    slot = lax.broadcasted_iota(jnp.int32, pre.shape, 0)
    message = jnp.where(slot < live_ref[0], pre * sigmoid(pre), 0.0).astype(BF)
    partial = mm(to_receiver, message).astype(BF)
    blocks = cn // crow
    for cb in range(width // ccol):
        cbuf[pl.ds(cb * blocks, blocks)] = partial[:, cb * ccol:(cb + 1) * ccol].reshape(blocks, crow, ccol)

    pl.semaphore_wait(barrier, n - 1)
    halo = [
        remote(outgoing.at[1], lookup.at[pl.ds(rows, send)], halo_ssem.at[0], halo_rsem.at[0], nxt),
        remote(outgoing.at[0], lookup.at[pl.ds(rows + send, send)], halo_ssem.at[1], halo_rsem.at[1], prv),
    ]
    for copy in halo:
        copy.start()

    def send_partial(o, c):
        to = lax.rem(me + o, n)
        remote(cbuf.at[to], crecv.at[o - 1], c_sem.at[0], c_sem.at[1], dev(to)).start()
        return c

    lax.fori_loop(1, n, send_partial, 0)

    loads[2].wait()
    source[pl.ds(0, rows), :] = mm(fine, msgw[:width, :]).astype(BF)
    target = mm(fine, msgw[width:, :]) + mbias_ref[...]
    local[...] = target
    for k in range(deg):
        pick[:, k * rows:(k + 1) * rows] = onehot_rows(table, nb_ref[k:k + 1, :])

    loads[3].wait()
    first = mm(fine, nodew[:width, :]) + nbias_ref[...]
    for copy in halo:
        copy.wait_recv()
    source[pl.ds(rows, table - rows), :] = mm(lookup[pl.ds(rows, table - rows), :], msgw[:width, :]).astype(BF)
    nb = jnp.concatenate([nb_ref[...], nb_ref[0:8 - deg, :]], 0)
    nb_col = nb.astype(F32).T.astype(jnp.int32)
    tile = rows // 2
    parts = []
    for t in range(2):
        agg = jnp.zeros((tile, width), F32)
        tgt = local[pl.ds(t * tile, tile), :]
        at = lax.broadcasted_iota(jnp.int32, (tile, table), 1)
        for k in range(deg):
            col = nb_col[t * tile:(t + 1) * tile, k:k + 1]
            hot = jnp.where(at == col, 1.0, 0.0).astype(BF)
            v = mm(hot, source[...]) + tgt
            filled = jnp.where(col < table, 1.0, 0.0)
            s = sigmoid(v) * filled
            silu = v * s
            agg = agg + silu
            slopes[k, pl.ds(t * tile, tile), :] = s + silu * (1.0 - s)
        parts.append(agg.astype(BF))
        if t == 0:
            remote(crecv, crecv, c_sem.at[0], c_sem.at[1], partner).wait_recv()
            share = jnp.sum(crecv[...].astype(F32), axis=0) + cbuf[me].astype(F32)
            cag[me] = share.astype(BF)

            def send_share(o, c):
                remote(cag.at[me], cag.at[me], c_sem.at[2], c_sem.at[3], dev(lax.rem(me + o, n))).start()
                return c

            lax.fori_loop(1, n, send_share, 0)
    aggregated = jnp.concatenate(parts, 0)

    first = first + mm(aggregated, nodew[width:2 * width, :])
    loads[4].wait()
    remote(crecv, crecv, c_sem.at[2], c_sem.at[3], partner).wait_recv()
    summed = jnp.concatenate(
        [cag[pl.ds(cb * blocks, blocks)].reshape(cn, ccol) for cb in range(width // ccol)], 1
    )
    hidden = mm(coarse, cnw[:width, :]) + mm(summed, cnw[width:, :]) + cnbias_ref[...]
    new_coarse = (coarse.astype(F32) + hidden * sigmoid(hidden)).astype(BF)
    newcoarse_ref[...] = new_coarse

    lifted = mm_tn(onehot_rows(cn, parent_ref[...]), new_coarse).astype(BF)
    node_pre = first + mm(lifted, nodew[2 * width:, :])
    real = lax.broadcasted_iota(jnp.int32, (rows, width), 0) < real_ref[0]
    s = sigmoid(node_pre)
    silu = node_pre * s
    newfine_ref[...] = jnp.where(real, fine.astype(F32) + silu, 0.0).astype(BF)
    loads[5].wait()
    out_grad = og[...].astype(F32)
    node_delta = jnp.where(real, out_grad * (s + silu * (1.0 - s)), 0.0).astype(BF)
    back = mm_nt(node_delta, nodew[width:2 * width, :])
    total = jnp.zeros((rows, width), F32)
    for k in range(deg):
        ed = (back * slopes[k]).astype(BF)
        edelta[pl.ds(k * rows, rows), :] = ed
        total = total + ed.astype(F32)
    dsum[...] = total.astype(BF)

    def keep(grad, which):
        for i in range(width // rpc):
            for j in range(cut):
                gbuf[which, i * cut + j] = grad[i * rpc:(i + 1) * rpc, j * cpc:(j + 1) * cpc]

    swap = remote(gbuf.at[1 - par], recv_a, g_sem.at[0], g_sem.at[1], partner)

    def scatter(which):
        swap.wait_recv()
        sum_b[...] = (gbuf[which].astype(F32) + recv_a[...].astype(F32)).astype(BF)

        def send_chunk(o, c):
            to = lax.rem(group + o, half)
            remote(sum_b.at[to], recv_b.at[o - 1], g_sem.at[2], g_sem.at[3], dev(2 * to + par)).start()
            return c

        lax.fori_loop(1, half, send_chunk, 0)

    def reduce(which):
        remote(recv_b, recv_b, g_sem.at[2], g_sem.at[3], partner).wait_recv()
        chunk = jnp.sum(recv_b[...].astype(F32), axis=0) + sum_b[group].astype(F32)
        ag[which, group] = chunk.astype(BF)
        mine = ag.at[which, group]
        remote(mine, mine, g_sem.at[5], g_sem.at[6], partner).start()

        def send_sum(o, c):
            to = lax.rem(group + o, half)
            remote(mine, mine, g_sem.at[4], ag_sem.at[o], dev(2 * to + par)).start()
            return c

        lax.fori_loop(1, half, send_sum, 0)

    def forward(which):
        def pass_on(o, c):
            got = ag.at[which, lax.rem(group + half - o, half)]
            remote(got, got, g_sem.at[4], ag_sem.at[o], partner).wait_recv()
            remote(got, got, g_sem.at[5], g_sem.at[6], partner).start()
            return c

        lax.fori_loop(1, half, pass_on, 0)

    odd, even = par == 1, par == 0
    keep(mm_tn(fine, dsum[...]).astype(BF), 1)

    @pl.when(even)
    def _():
        swap.start()

    tdelta[pl.ds(rows, table - rows), :] = mm(pick[pl.ds(rows, table - rows), :], edelta[...]).astype(BF)
    rim = mm_nt(tdelta[pl.ds(rows, table - rows), :], msgw[:width, :]).astype(BF)
    retout[0] = rim[:send]
    retout[1] = rim[send:]
    give = [
        remote(retout.at[1], ret.at[0], halo_ssem.at[2], halo_rsem.at[2], nxt),
        remote(retout.at[0], ret.at[1], halo_ssem.at[3], halo_rsem.at[3], prv),
    ]
    for copy in give:
        copy.start()

    @pl.when(odd)
    def _():
        scatter(1)

    tdelta[pl.ds(0, rows), :] = mm(pick[pl.ds(0, rows), :], edelta[...]).astype(BF)
    keep(mm_tn(lookup[...], tdelta[...]).astype(BF), 0)

    @pl.when(odd)
    def _():
        swap.start()

    local[...] = out_grad + mm_nt(node_delta, nodew[:width, :])

    @pl.when(even)
    def _():
        scatter(0)

    @pl.when(odd)
    def _():
        reduce(1)

    grad = local[...] + mm_nt(dsum[...], msgw[width:, :]) + mm_nt(tdelta[pl.ds(0, rows), :], msgw[:width, :])
    for copy in give:
        copy.wait_recv()
    grad = grad + mm(sends_oh[:, :send], ret[0]) + mm(sends_oh[:, send:], ret[1])
    nodegrad_ref[...] = jnp.where(real, grad, 0.0).astype(BF)

    @pl.when(even)
    def _():
        reduce(0)
        forward(0)

    @pl.when(odd)
    def _():
        forward(1)

    whole_half = remote(recv_a, recv_a, g_sem.at[5], g_sem.at[6], partner)
    whole_half.wait_recv()
    out = pltpu.make_async_copy(ag, raw_hbm, out_sem)
    out.start()
    raw = ag[...].astype(F32)
    mean = jnp.sum(raw * raw) / (2 * width * width)
    factor_ref[...] = jnp.full(factor_ref.shape, lax.rsqrt(mean + epsilon), F32)

    for copy in halo + give:
        copy.wait_send()
    remote(crecv, crecv, c_sem.at[0], c_sem.at[1], partner).wait_send()
    remote(crecv, crecv, c_sem.at[2], c_sem.at[3], partner).wait_send()
    swap.wait_send()
    remote(recv_b, recv_b, g_sem.at[2], g_sem.at[3], partner).wait_send()
    remote(recv_b, recv_b, g_sem.at[4], g_sem.at[3], partner).wait_send()
    whole_half.wait_send()
    out.wait()


def shards(
    patches, subs,
    fine_nodes, coarse_nodes, neighbours, send_rows, real_rows, parent,
    coarse_edges, coarse_live, msg_weight, msg_bias, node_weight, node_bias,
    coarse_msg_weight, coarse_msg_bias, coarse_node_weight, coarse_node_bias,
    out_grad,
):
    n = patches * subs
    half = n // 2
    rows, width = fine_nodes.shape
    send = send_rows.shape[2]
    table = rows + 2 * send
    deg = neighbours.shape[0]
    cn = coarse_nodes.shape[0]
    cut = max(1, 16 * n // (2 * width))
    rpc, cpc = 2 * width * cut // n, width // cut
    ccol = 128
    crow = cn * (width // ccol) // n
    vmem = pl.BlockSpec(memory_space=pltpu.VMEM)
    smem = pl.BlockSpec(memory_space=pltpu.SMEM)
    hbm = pl.BlockSpec(memory_space=pl.ANY)
    V = pltpu.VMEM
    dma = pltpu.SemaphoreType.DMA
    new_fine, new_coarse, node_grad, raw, factor = pl.pallas_call(
        functools.partial(layer_kernel, patches, subs, cut),
        out_shape=(
            jax.ShapeDtypeStruct((rows, width), BF),
            jax.ShapeDtypeStruct((cn, width), BF),
            jax.ShapeDtypeStruct((rows, width), BF),
            jax.ShapeDtypeStruct((2, half, rpc, cpc), BF),
            jax.ShapeDtypeStruct((1, width), F32),
        ),
        in_specs=[smem, smem] + [vmem] * 9 + [hbm] * 6,
        out_specs=(vmem, vmem, vmem, hbm, vmem),
        scratch_shapes=[
            V((table, width), BF), V((2 * width, width), BF), V((3 * width, width), BF),
            V((2 * width, width), BF), V((2 * width, width), BF), V((rows, width), BF), dma((6,)),
            V((2, send, width), BF), V((2, send, width), BF), V((2, send, width), BF), dma((4,)), dma((4,)),
            V((n, crow, ccol), BF), V((n - 1, crow, ccol), BF), V((n, crow, ccol), BF), dma((4,)),
            V((table, deg * rows), BF), V((deg, rows, width), F32), V((deg * rows, width), BF),
            V((table, width), BF), V((table, width), BF), V((rows, width), BF),
            V((rows, width), F32), V((rows, 2 * send), BF),
            V((2, half, rpc, cpc), BF), V((half, rpc, cpc), BF), V((half, rpc, cpc), BF),
            V((half - 1, rpc, cpc), BF), V((2, half, rpc, cpc), BF), dma((8,)), dma((half,)), dma,
        ],
        compiler_params=pltpu.CompilerParams(
            collective_id=0, has_side_effects=True, vmem_limit_bytes=56 * 1024 * 1024
        ),
        name="layer",
    )(
        real_rows, coarse_live, neighbours, send_rows[0], parent[None, :], coarse_edges, coarse_nodes,
        msg_bias[None, :], node_bias[None, :], coarse_msg_bias[None, :], coarse_node_bias[None, :],
        fine_nodes, msg_weight, node_weight, coarse_msg_weight, coarse_node_weight, out_grad,
    )
    if cut > 1:
        raw = raw.reshape(2 * width // rpc, cut, rpc, cpc).transpose(0, 2, 1, 3)
    msg_weight_grad = raw.reshape(2 * width, width).astype(F32) * factor
    return new_fine, new_coarse, node_grad, msg_weight_grad


def solution(mesh):
    both = P(AXES)
    placed = (
        P(AXES, None), P(), P(None, AXES), P(AXES, None, None), both, both, P(None, AXES), both,
        P(), P(), P(), P(), P(), P(), P(), P(), P(AXES, None),
    )
    return jax.shard_map(
        functools.partial(shards, mesh.shape["patch"], mesh.shape["sub"]),
        mesh=mesh,
        in_specs=placed,
        out_specs=(P(AXES, None), P(), P(AXES, None), P()),
        check_vma=False,
    )
```

```python
import functools

import jax
import jax.numpy as jnp
from jax import lax
from jax.experimental import pallas as pl
from jax.experimental.pallas import tpu as pltpu
from jax.sharding import PartitionSpec as P

MESH = pl.DeviceIdType.MESH
AXES = ("patch", "sub")
epsilon = 1e-06
BF = jnp.bfloat16
F32 = jnp.float32


def mm(a, b):
    return jnp.dot(a, b, preferred_element_type=F32)


def mm_nt(a, b):
    return lax.dot_general(a, b, (((1,), (1,)), ((), ())), preferred_element_type=F32)


def mm_tn(a, b):
    return lax.dot_general(a, b, (((0,), (0,)), ((), ())), preferred_element_type=F32)


def sigmoid(v):
    return 0.5 + 0.5 * jnp.tanh(0.5 * v)


def onehot_rows(count, row):
    at = lax.broadcasted_iota(jnp.int32, (count, row.shape[1]), 0)
    return jnp.where(at == row, 1.0, 0.0).astype(BF)


def layer_kernel(
    patches, subs, cut,
    real_ref, live_ref, nb_ref, send_ref, parent_ref, edges_ref, coarse_ref,
    mbias_ref, nbias_ref, cmbias_ref, cnbias_ref,
    fine_hbm, msgw_hbm, nodew_hbm, cmw_hbm, cnw_hbm, og_hbm,
    newfine_ref, newcoarse_ref, nodegrad_ref, raw_hbm, factor_ref,
    lookup, msgw, nodew, cmw, cnw, og, load_sem,
    outgoing, ret, retout, halo_ssem, halo_rsem,
    cbuf, crecv, cag, c_sem,
    pick, slopes, edelta, source, tdelta, dsum, local, sends_oh,
    gbuf, recv_a, sum_b, recv_b, sum_c, recv_c, ag, g_sem, ag_sem, out_sem,
):
    n = patches * subs
    half = n // 2
    rows, width = og.shape
    send = outgoing.shape[1]
    table = lookup.shape[0]
    deg = nb_ref.shape[0]
    cn = coarse_ref.shape[0]
    _, _, rpc, cpc = gbuf.shape
    crow, ccol = cbuf.shape[1:]
    me = lax.axis_index("patch") * subs + lax.axis_index("sub")
    par = lax.rem(me, 2)
    lo = ag_sem.shape[0]
    hi = half // lo
    high, low = lax.div(me, 2 * lo), lax.rem(lax.div(me, 2), lo)

    def dev(i):
        return (lax.div(i, subs), lax.rem(i, subs))

    partner = dev(me + 1 - 2 * par)
    nxt, prv = dev(lax.rem(me + 1, n)), dev(lax.rem(me + n - 1, n))

    def remote(src, dst, ssem, rsem, to):
        return pltpu.make_async_remote_copy(
            src_ref=src, dst_ref=dst, send_sem=ssem, recv_sem=rsem,
            device_id=to, device_id_type=MESH,
        )

    barrier = pltpu.get_barrier_semaphore()

    def greet(o, c):
        pl.semaphore_signal(barrier, inc=1, device_id=dev(lax.rem(me + o, n)), device_id_type=MESH)
        return c

    loads = [
        pltpu.make_async_copy(fine_hbm, lookup.at[pl.ds(0, rows)], load_sem.at[0]),
        pltpu.make_async_copy(cmw_hbm, cmw, load_sem.at[1]),
        pltpu.make_async_copy(msgw_hbm, msgw, load_sem.at[2]),
        pltpu.make_async_copy(nodew_hbm, nodew, load_sem.at[3]),
        pltpu.make_async_copy(cnw_hbm, cnw, load_sem.at[4]),
        pltpu.make_async_copy(og_hbm, og, load_sem.at[5]),
    ]
    for load in loads:
        load.start()
    lax.fori_loop(1, n, greet, 0)

    sends_oh[:, :send] = onehot_rows(rows, send_ref[0:1, :])
    sends_oh[:, send:] = onehot_rows(rows, send_ref[1:2, :])
    loads[0].wait()
    fine = lookup[pl.ds(0, rows), :]
    gathered = mm_tn(sends_oh[...], fine).astype(BF)
    outgoing[0] = gathered[:send]
    outgoing[1] = gathered[send:]
    coarse = coarse_ref[...]
    to_sender = onehot_rows(cn, edges_ref[0:1, :])
    to_receiver = onehot_rows(cn, edges_ref[1:2, :])
    senders = mm_tn(to_sender, coarse).astype(BF)
    receivers = mm_tn(to_receiver, coarse).astype(BF)
    loads[1].wait()
    pre = mm(senders, cmw[:width, :]) + mm(receivers, cmw[width:, :]) + cmbias_ref[...]
    slot = lax.broadcasted_iota(jnp.int32, pre.shape, 0)
    message = jnp.where(slot < live_ref[0], pre * sigmoid(pre), 0.0).astype(BF)
    partial = mm(to_receiver, message).astype(BF)
    blocks = cn // crow
    for cb in range(width // ccol):
        cbuf[pl.ds(cb * blocks, blocks)] = partial[:, cb * ccol:(cb + 1) * ccol].reshape(blocks, crow, ccol)

    pl.semaphore_wait(barrier, n - 1)
    halo = [
        remote(outgoing.at[1], lookup.at[pl.ds(rows, send)], halo_ssem.at[0], halo_rsem.at[0], nxt),
        remote(outgoing.at[0], lookup.at[pl.ds(rows + send, send)], halo_ssem.at[1], halo_rsem.at[1], prv),
    ]
    for copy in halo:
        copy.start()

    def send_partial(o, c):
        to = lax.rem(me + o, n)
        remote(cbuf.at[to], crecv.at[o - 1], c_sem.at[0], c_sem.at[1], dev(to)).start()
        return c

    lax.fori_loop(1, n, send_partial, 0)

    loads[2].wait()
    source[pl.ds(0, rows), :] = mm(fine, msgw[:width, :]).astype(BF)
    target = mm(fine, msgw[width:, :]) + mbias_ref[...]
    local[...] = target
    for k in range(deg):
        pick[:, k * rows:(k + 1) * rows] = onehot_rows(table, nb_ref[k:k + 1, :])

    loads[3].wait()
    first = mm(fine, nodew[:width, :]) + nbias_ref[...]
    for copy in halo:
        copy.wait_recv()
    source[pl.ds(rows, table - rows), :] = mm(lookup[pl.ds(rows, table - rows), :], msgw[:width, :]).astype(BF)
    nb = jnp.concatenate([nb_ref[...], nb_ref[0:8 - deg, :]], 0)
    nb_col = nb.astype(F32).T.astype(jnp.int32)
    tile = rows // 2
    parts = []
    for t in range(2):
        agg = jnp.zeros((tile, width), F32)
        tgt = local[pl.ds(t * tile, tile), :]
        at = lax.broadcasted_iota(jnp.int32, (tile, table), 1)
        for k in range(deg):
            col = nb_col[t * tile:(t + 1) * tile, k:k + 1]
            hot = jnp.where(at == col, 1.0, 0.0).astype(BF)
            v = mm(hot, source[...]) + tgt
            filled = jnp.where(col < table, 1.0, 0.0)
            s = sigmoid(v) * filled
            silu = v * s
            agg = agg + silu
            slopes[k, pl.ds(t * tile, tile), :] = s + silu * (1.0 - s)
        parts.append(agg.astype(BF))
        if t == 0:
            remote(crecv, crecv, c_sem.at[0], c_sem.at[1], partner).wait_recv()
            share = jnp.sum(crecv[...].astype(F32), axis=0) + cbuf[me].astype(F32)
            cag[me] = share.astype(BF)

            def send_share(o, c):
                remote(cag.at[me], cag.at[me], c_sem.at[2], c_sem.at[3], dev(lax.rem(me + o, n))).start()
                return c

            lax.fori_loop(1, n, send_share, 0)
    aggregated = jnp.concatenate(parts, 0)

    first = first + mm(aggregated, nodew[width:2 * width, :])
    loads[4].wait()
    remote(crecv, crecv, c_sem.at[2], c_sem.at[3], partner).wait_recv()
    summed = jnp.concatenate(
        [cag[pl.ds(cb * blocks, blocks)].reshape(cn, ccol) for cb in range(width // ccol)], 1
    )
    hidden = mm(coarse, cnw[:width, :]) + mm(summed, cnw[width:, :]) + cnbias_ref[...]
    new_coarse = (coarse.astype(F32) + hidden * sigmoid(hidden)).astype(BF)
    newcoarse_ref[...] = new_coarse

    lifted = mm_tn(onehot_rows(cn, parent_ref[...]), new_coarse).astype(BF)
    node_pre = first + mm(lifted, nodew[2 * width:, :])
    real = lax.broadcasted_iota(jnp.int32, (rows, width), 0) < real_ref[0]
    s = sigmoid(node_pre)
    silu = node_pre * s
    newfine_ref[...] = jnp.where(real, fine.astype(F32) + silu, 0.0).astype(BF)
    loads[5].wait()
    out_grad = og[...].astype(F32)
    node_delta = jnp.where(real, out_grad * (s + silu * (1.0 - s)), 0.0).astype(BF)
    back = mm_nt(node_delta, nodew[width:2 * width, :])
    total = jnp.zeros((rows, width), F32)
    for k in range(deg):
        ed = (back * slopes[k]).astype(BF)
        edelta[pl.ds(k * rows, rows), :] = ed
        total = total + ed.astype(F32)
    dsum[...] = total.astype(BF)

    def keep(grad, which):
        for i in range(width // rpc):
            for j in range(cut):
                gbuf[which, i * cut + j] = grad[i * rpc:(i + 1) * rpc, j * cpc:(j + 1) * cpc]

    swap = remote(gbuf.at[1 - par], recv_a, g_sem.at[0], g_sem.at[1], partner)

    def scatter(which):
        swap.wait_recv()
        sum_b[...] = (gbuf[which].astype(F32) + recv_a[...].astype(F32)).astype(BF)

        for o in range(1, lo):
            to = lax.rem(low + o, lo)
            remote(
                sum_b.at[pl.ds(to * hi, hi)], recv_b.at[o - 1],
                g_sem.at[2], g_sem.at[3], dev(2 * (high * lo + to) + par),
            ).start()

    def line(which):
        remote(recv_b, recv_b, g_sem.at[2], g_sem.at[3], partner).wait_recv()
        own = sum_b[pl.ds(low * hi, hi)].astype(F32) + jnp.sum(recv_b[...].astype(F32), axis=0)
        sum_c[...] = own.astype(BF)

        def send_chunk(o, c):
            to = lax.rem(high + o, hi)
            remote(
                sum_c.at[to], recv_c.at[o - 1],
                g_sem.at[7], g_sem.at[8], dev(2 * (to * lo + low) + par),
            ).start()
            return c

        lax.fori_loop(1, hi, send_chunk, 0)

    def reduce(which):
        remote(recv_c, recv_c, g_sem.at[7], g_sem.at[8], partner).wait_recv()
        chunk = jnp.sum(recv_c[...].astype(F32), axis=0) + sum_c[high].astype(F32)
        mine = ag.at[which, low * hi + high]
        ag[which, low * hi + high] = chunk.astype(BF)

        def send_sum(o, c):
            to = lax.rem(high + o, hi)
            remote(mine, mine, g_sem.at[4], g_sem.at[9], dev(2 * (to * lo + low) + par)).start()
            return c

        lax.fori_loop(1, hi, send_sum, 0)

    def spread(which):
        remote(recv_c, recv_c, g_sem.at[4], g_sem.at[9], partner).wait_recv()
        block = ag.at[which, pl.ds(low * hi, hi)]
        for o in range(1, lo):
            to = lax.rem(low + o, lo)
            remote(block, block, g_sem.at[10], ag_sem.at[o], dev(2 * (high * lo + to) + par)).start()
        remote(block, block, g_sem.at[5], g_sem.at[6], partner).start()

    def forward(which):
        for o in range(1, lo):
            got = ag.at[which, pl.ds(lax.rem(low + lo - o, lo) * hi, hi)]
            remote(got, got, g_sem.at[10], ag_sem.at[o], partner).wait_recv()
            remote(got, got, g_sem.at[5], g_sem.at[6], partner).start()

    odd, even = par == 1, par == 0
    keep(mm_tn(fine, dsum[...]).astype(BF), 1)

    @pl.when(even)
    def _():
        swap.start()

    tdelta[pl.ds(rows, table - rows), :] = mm(pick[pl.ds(rows, table - rows), :], edelta[...]).astype(BF)
    rim = mm_nt(tdelta[pl.ds(rows, table - rows), :], msgw[:width, :]).astype(BF)
    retout[0] = rim[:send]
    retout[1] = rim[send:]
    give = [
        remote(retout.at[1], ret.at[0], halo_ssem.at[2], halo_rsem.at[2], nxt),
        remote(retout.at[0], ret.at[1], halo_ssem.at[3], halo_rsem.at[3], prv),
    ]
    for copy in give:
        copy.start()

    @pl.when(odd)
    def _():
        scatter(1)

    tdelta[pl.ds(0, rows), :] = mm(pick[pl.ds(0, rows), :], edelta[...]).astype(BF)
    keep(mm_tn(lookup[...], tdelta[...]).astype(BF), 0)

    @pl.when(odd)
    def _():
        swap.start()
        line(1)

    local[...] = out_grad + mm_nt(node_delta, nodew[:width, :])

    @pl.when(even)
    def _():
        scatter(0)

    @pl.when(odd)
    def _():
        reduce(1)

    local[...] += mm_nt(dsum[...], msgw[width:, :])
    grad = local[...] + mm_nt(tdelta[pl.ds(0, rows), :], msgw[:width, :])

    @pl.when(odd)
    def _():
        spread(1)

    @pl.when(even)
    def _():
        line(0)

    for copy in give:
        copy.wait_recv()
    grad = grad + mm(sends_oh[:, :send], ret[0]) + mm(sends_oh[:, send:], ret[1])
    nodegrad_ref[...] = jnp.where(real, grad, 0.0).astype(BF)

    @pl.when(even)
    def _():
        reduce(0)
        spread(0)
        forward(0)

    @pl.when(odd)
    def _():
        forward(1)

    whole_half = remote(recv_a, recv_a, g_sem.at[5], g_sem.at[6], partner)
    whole_half.wait_recv()
    out = pltpu.make_async_copy(ag, raw_hbm, out_sem)
    out.start()
    raw = ag[...].astype(F32)
    mean = jnp.sum(raw * raw) / (2 * width * width)
    factor_ref[...] = jnp.full(factor_ref.shape, lax.rsqrt(mean + epsilon), F32)

    for copy in halo + give:
        copy.wait_send()
    remote(crecv, crecv, c_sem.at[0], c_sem.at[1], partner).wait_send()
    remote(crecv, crecv, c_sem.at[2], c_sem.at[3], partner).wait_send()
    swap.wait_send()
    remote(recv_b, recv_b, g_sem.at[2], g_sem.at[3], partner).wait_send()
    remote(recv_c, recv_c, g_sem.at[7], g_sem.at[8], partner).wait_send()
    remote(recv_c, recv_c, g_sem.at[4], g_sem.at[9], partner).wait_send()
    remote(recv_b, recv_b, g_sem.at[10], g_sem.at[3], partner).wait_send()
    whole_half.wait_send()
    out.wait()


def shards(
    patches, subs,
    fine_nodes, coarse_nodes, neighbours, send_rows, real_rows, parent,
    coarse_edges, coarse_live, msg_weight, msg_bias, node_weight, node_bias,
    coarse_msg_weight, coarse_msg_bias, coarse_node_weight, coarse_node_bias,
    out_grad,
):
    n = patches * subs
    half = n // 2
    lo = 4
    hi = half // lo
    rows, width = fine_nodes.shape
    send = send_rows.shape[2]
    table = rows + 2 * send
    deg = neighbours.shape[0]
    cn = coarse_nodes.shape[0]
    cut = max(1, 16 * n // (2 * width))
    rpc, cpc = 2 * width * cut // n, width // cut
    ccol = 128
    crow = cn * (width // ccol) // n
    vmem = pl.BlockSpec(memory_space=pltpu.VMEM)
    smem = pl.BlockSpec(memory_space=pltpu.SMEM)
    hbm = pl.BlockSpec(memory_space=pl.ANY)
    V = pltpu.VMEM
    dma = pltpu.SemaphoreType.DMA
    new_fine, new_coarse, node_grad, raw, factor = pl.pallas_call(
        functools.partial(layer_kernel, patches, subs, cut),
        out_shape=(
            jax.ShapeDtypeStruct((rows, width), BF),
            jax.ShapeDtypeStruct((cn, width), BF),
            jax.ShapeDtypeStruct((rows, width), BF),
            jax.ShapeDtypeStruct((2, half, rpc, cpc), BF),
            jax.ShapeDtypeStruct((1, width), F32),
        ),
        in_specs=[smem, smem] + [vmem] * 9 + [hbm] * 6,
        out_specs=(vmem, vmem, vmem, hbm, vmem),
        scratch_shapes=[
            V((table, width), BF), V((2 * width, width), BF), V((3 * width, width), BF),
            V((2 * width, width), BF), V((2 * width, width), BF), V((rows, width), BF), dma((6,)),
            V((2, send, width), BF), V((2, send, width), BF), V((2, send, width), BF), dma((4,)), dma((4,)),
            V((n, crow, ccol), BF), V((n - 1, crow, ccol), BF), V((n, crow, ccol), BF), dma((4,)),
            V((table, deg * rows), BF), V((deg, rows, width), F32), V((deg * rows, width), BF),
            V((table, width), BF), V((table, width), BF), V((rows, width), BF),
            V((rows, width), F32), V((rows, 2 * send), BF),
            V((2, half, rpc, cpc), BF), V((half, rpc, cpc), BF), V((half, rpc, cpc), BF),
            V((lo - 1, hi, rpc, cpc), BF), V((hi, rpc, cpc), BF), V((hi - 1, rpc, cpc), BF), V((2, half, rpc, cpc), BF), dma((11,)), dma((lo,)), dma,
        ],
        compiler_params=pltpu.CompilerParams(
            collective_id=0, has_side_effects=True, vmem_limit_bytes=56 * 1024 * 1024
        ),
        name="layer",
    )(
        real_rows, coarse_live, neighbours, send_rows[0], parent[None, :], coarse_edges, coarse_nodes,
        msg_bias[None, :], node_bias[None, :], coarse_msg_bias[None, :], coarse_node_bias[None, :],
        fine_nodes, msg_weight, node_weight, coarse_msg_weight, coarse_node_weight, out_grad,
    )
    if cut > 1:
        raw = raw.reshape(2 * width // rpc, cut, rpc, cpc).transpose(0, 2, 1, 3)
    msg_weight_grad = raw.reshape(2 * width, width).astype(F32) * factor
    return new_fine, new_coarse, node_grad, msg_weight_grad


def solution(mesh):
    both = P(AXES)
    placed = (
        P(AXES, None), P(), P(None, AXES), P(AXES, None, None), both, both, P(None, AXES), both,
        P(), P(), P(), P(), P(), P(), P(), P(), P(AXES, None),
    )
    return jax.shard_map(
        functools.partial(shards, mesh.shape["patch"], mesh.shape["sub"]),
        mesh=mesh,
        in_specs=placed,
        out_specs=(P(AXES, None), P(), P(AXES, None), P()),
        check_vma=False,
    )
```
